512 devices in a mesh: section: 32 (over y, z_hi), dp: 16 (over x, z_lo, core).
Axes of the slice: x: 4, y: 8, z: 8 (z_hi: 4, z_lo: 2; z = z_hi * 2 + z_lo), core: 2. Of those that a mesh axis runs over, the one named last changes fastest.
Arguments:
- inputs: bfloat16 [768, 8192], P(None, 'dp'), may hold values from -6 to 6
- out_grad: bfloat16 [768, 8192], P(None, 'dp'), may hold values from -6 to 6
- saved_codes: int32 [768, 32768], P('dp', 'section'), may hold values from -127 to 127
- row_scale: float32 [768], P('dp'), may hold values from 0.005 to 0.04
- w_in: bfloat16 [8192, 32768], P('dp', 'section'), may hold values from -0.0625 to 0.0625
- w_out: bfloat16 [32768, 8192], P('section', 'dp'), may hold values from -0.03125 to 0.03125
Outputs:
- input_grad: bfloat16 [768, 8192], P('section', 'dp')
- w_in_grad: bfloat16 [8192, 32768], P('dp', 'section')
- w_out_grad: bfloat16 [32768, 8192], P('section', 'dp')
The draws below stay inside these ranges and needn't reach their ends.
All inputs are finite; a program needn't handle non-finite values.
Results may differ from the reference program's by a relative error of at most 0.015.
Values may be sent and summed in bfloat16 or wider, within the bound.
No kernel may reach another device: no remote copies, remote signals or barrier semaphores. Data moves between devices by JAX's collectives and lax.ppermute only.
A program may use at most 64 MiB of HBM per device.

```python
import math
import jax
import jax.numpy as jnp
from jax import lax

D = 8192
FF = 32768
TOKENS = 768


def set_ends(array, rng, low, largest):
    longest = array.shape.index(max(array.shape))
    spots = []
    for shift in (0, 1):
        where = [jax.random.randint(jax.random.fold_in(rng, axis), (), 0, length) for axis, length in enumerate(array.shape)]
        where[longest] = (where[longest] + shift) % array.shape[longest]
        spots.append(tuple(where))
    return array.at[spots[0]].set(low).at[spots[1]].set(largest)


def with_spikes(result, stream_key, source, target, blocks, factor):
    owner, partner = [(jnp.arange(result.shape[dim]) // (result.shape[dim] // blocks)).reshape([-1 if axis == dim else 1 for axis in range(result.ndim)]) for dim in (source, target)]
    chosen = jax.random.permutation(stream_key, blocks)[partner]
    strong = (owner == chosen) | (owner == (partner + blocks // 2) % blocks)
    return jnp.where(strong, factor * result, result)


def levels(own_key, shape, split, least, high):
    level = 1.0
    for position, shards_of in split:
        draws = jax.random.uniform(jax.random.fold_in(jax.random.fold_in(own_key, 6), position), (shards_of,), jnp.float32, least / len(split), high / len(split))
        level = level * jnp.repeat(jnp.exp(draws), shape[position] // shards_of).reshape((-1,) + (1,) * (len(shape) - 1 - position))
    return level


def scatter_about(rng, shape, spread, limit, shards=(), held_as=jnp.bfloat16):
    level = levels(rng, shape, shards, -0.22, 0.18) if shards else 1.0
    entries = jax.random.normal(rng, shape, jnp.float32) * spread * level
    return jnp.minimum(jnp.maximum(entries, -limit), limit).astype(held_as)


def noise_with(own_key, dims, scale, bound, split, heavy, kind=jnp.bfloat16):
    array = scale * jax.random.normal(own_key, dims, jnp.float32)
    if split:
        array = array * levels(own_key, dims, split, -0.22, 0.18)
    return jnp.clip(with_spikes(array, jax.random.fold_in(own_key, 3), *heavy), -bound, bound).astype(kind)


def setup_inputs(seed: int = 0) -> dict:
    streams_of = jax.random.split(jax.random.key(seed), 7)
    return {
        "inputs": scatter_about(streams_of[0], (TOKENS, D), 1.0, 6.0, ((1, 16),)),
        "out_grad": noise_with(streams_of[1], (TOKENS, D), 1.0, 6.0, ((1, 16),), (1, 0, 16, 2.0)),
        "saved_codes": set_ends(jax.random.randint(streams_of[2], (TOKENS, FF), -127, 128), jax.random.fold_in(streams_of[2], 1), -127, 127).astype(jnp.int32),
        "row_scale": jnp.clip(jnp.exp(math.log(0.04) - 2.0794415 * jax.random.uniform(streams_of[3], (TOKENS,), jnp.float32) ** levels(streams_of[3], (TOKENS,), ((0, 16),), -0.2, 0.2)), 0.005, 0.04),
        "w_in": scatter_about(streams_of[4], (D, FF), D ** -0.5, 0.0625, ((0, 16), (1, 32))),
        "w_out": scatter_about(streams_of[5], (FF, D), FF ** -0.5, 0.03125, ((0, 32), (1, 16))),
    }


inv_root_two = 1.0 / math.sqrt(2.0)
inv_root_tau = 1.0 / math.sqrt(2.0 * math.pi)

def reference(inputs, out_grad, saved_codes, row_scale, w_in, w_out):
    pre_act = saved_codes.astype(jnp.float32) * row_scale[:, None]
    normal_cdf = 0.5 * (1.0 + jax.scipy.special.erf(pre_act * inv_root_two))
    hidden = (pre_act * normal_cdf).astype(jnp.bfloat16)
    slope = (normal_cdf + pre_act * jnp.exp(-0.5 * pre_act * pre_act) * inv_root_tau).astype(jnp.bfloat16)
    hidden_grad = lax.dot_general(out_grad, w_out, (((1,), (1,)), ((), ())), preferred_element_type=jnp.float32)
    pre_grad = (hidden_grad * slope).astype(jnp.bfloat16)
    input_grad = lax.dot_general(pre_grad, w_in, (((1,), (1,)), ((), ())), preferred_element_type=jnp.float32)
    w_in_grad = lax.dot_general(inputs, pre_grad, (((0,), (0,)), ((), ())), preferred_element_type=jnp.float32)
    w_out_grad = lax.dot_general(hidden, out_grad, (((0,), (0,)), ((), ())), preferred_element_type=jnp.float32)
    return (input_grad.astype(jnp.bfloat16), w_in_grad.astype(jnp.bfloat16), w_out_grad.astype(jnp.bfloat16))
```

```python
import math

import jax
import jax.numpy as jnp
from jax import lax
from jax.sharding import Mesh
from jax.sharding import PartitionSpec as P

inv_root_two = 1.0 / math.sqrt(2.0)
inv_root_tau = 1.0 / math.sqrt(2.0 * math.pi)

SECTION = ("y", "zh")
DP = ("x", "zl", "core")


def contract_last(left, right):
    return lax.dot_general(
        left, right, (((1,), (1,)), ((), ())), preferred_element_type=jnp.float32
    )


def contract_first(left, right):
    return lax.dot_general(
        left, right, (((0,), (0,)), ((), ())), preferred_element_type=jnp.float32
    )


def exchange_sum(part, axis, count):
    blocks = lax.all_to_all(part.astype(jnp.bfloat16), axis, 0, 0, tiled=True)
    rows = part.shape[0] // count
    return jnp.sum(blocks.reshape(count, rows, part.shape[1]).astype(jnp.float32), axis=0)


def body(inputs, out_grad, saved_codes, row_scale, w_in, w_out):
    pre_act = saved_codes.astype(jnp.float32) * row_scale[:, None]
    normal_cdf = 0.5 * (1.0 + jax.scipy.special.erf(pre_act * inv_root_two))
    hidden_own = (pre_act * normal_cdf).astype(jnp.bfloat16)
    slope_own = (normal_cdf + pre_act * jnp.exp(-0.5 * pre_act * pre_act) * inv_root_tau).astype(
        jnp.bfloat16
    )
    hidden = lax.all_gather(hidden_own, DP, axis=0, tiled=True)
    grad_share = exchange_sum(contract_last(out_grad, w_out), DP, 16)
    pre_grad_own = (grad_share * slope_own).astype(jnp.bfloat16)
    same_core = lax.all_to_all(
        jnp.tile(pre_grad_own, (8, 1)), ("x", "zl"), 0, 0, tiled=True
    )
    both = lax.all_to_all(jnp.tile(same_core, (2, 1)), "core", 0, 0, tiled=True)
    pre_grad = both.reshape(2, 8, 48, 1024).transpose(1, 0, 2, 3).reshape(768, 1024)
    input_grad = exchange_sum(contract_last(pre_grad, w_in), SECTION, 32)
    w_in_total = contract_first(inputs, pre_grad)
    w_out_total = contract_first(hidden, out_grad)
    return (
        input_grad.astype(jnp.bfloat16),
        w_in_total.astype(jnp.bfloat16),
        w_out_total.astype(jnp.bfloat16),
    )


def solution(mesh):
    cut = Mesh(mesh.devices.reshape(8, 4, 4, 2, 2), SECTION + DP)
    placed = (
        P(None, DP),
        P(None, DP),
        P(DP, SECTION),
        P(DP),
        P(DP, SECTION),
        P(SECTION, DP),
    )
    return jax.shard_map(
        body,
        mesh=cut,
        in_specs=placed,
        out_specs=(P(SECTION, DP), P(DP, SECTION), P(SECTION, DP)),
        check_vma=False,
    )
```

```python
import math

import jax
import jax.numpy as jnp
from jax import lax
from jax.sharding import Mesh
from jax.sharding import PartitionSpec as P

inv_root_two = 1.0 / math.sqrt(2.0)
inv_root_tau = 1.0 / math.sqrt(2.0 * math.pi)

SECTION = ("y", "zh")
CHIPS = ("x", "zl")
DP = ("x", "zl", "core")


def contract_last(left, right):
    return lax.dot_general(
        left, right, (((1,), (1,)), ((), ())), preferred_element_type=jnp.float32
    )


def contract_first(left, right):
    return lax.dot_general(
        left, right, (((0,), (0,)), ((), ())), preferred_element_type=jnp.float32
    )


def core_swap(block):
    return lax.ppermute(block, "core", [(0, 1), (1, 0)])


def split_cores(rows):
    me = lax.axis_index("core")
    cut = rows.reshape(8, 2, 48, rows.shape[1])
    mine = lax.dynamic_index_in_dim(cut, me, 1, keepdims=False)
    other = lax.dynamic_index_in_dim(cut, 1 - me, 1, keepdims=False)
    return mine.reshape(384, -1), other.reshape(384, -1)


def join_cores(mine, other):
    first = lax.axis_index("core") == 0
    mine, other = mine.reshape(8, 48, -1), other.reshape(8, 48, -1)
    both = jnp.stack([jnp.where(first, mine, other), jnp.where(first, other, mine)], axis=1)
    return both.reshape(768, -1)


def copies_to_chips(block):
    return lax.all_to_all(jnp.tile(block, (8, 1)), CHIPS, 0, 0, tiled=True)


def body(inputs, out_grad, saved_codes, row_scale, w_in, w_out):
    pre_act = saved_codes.astype(jnp.float32) * row_scale[:, None]
    normal_cdf = 0.5 * (1.0 + jax.scipy.special.erf(pre_act * inv_root_two))
    hidden_own = (pre_act * normal_cdf).astype(jnp.bfloat16)
    slope_own = (normal_cdf + pre_act * jnp.exp(-0.5 * pre_act * pre_act) * inv_root_tau).astype(
        jnp.bfloat16
    )
    hidden_own, slope_own = lax.optimization_barrier((hidden_own, slope_own))

    grad_mine, grad_other = split_cores(out_grad)
    received = core_swap(contract_last(grad_other, w_out).astype(jnp.bfloat16))
    own_sum = lax.optimization_barrier(contract_last(grad_mine, w_out))
    chip_sum = own_sum + received.astype(jnp.float32)
    blocks = lax.all_to_all(chip_sum.astype(jnp.bfloat16), CHIPS, 0, 0, tiled=True)
    hidden_pair = lax.all_gather(hidden_own, "zl", axis=0, tiled=True)
    blocks, hidden_pair = lax.optimization_barrier((blocks, hidden_pair))
    grad_share = jnp.sum(blocks.reshape(8, 48, 1024).astype(jnp.float32), axis=0)
    pre_grad_own = (grad_share * slope_own).astype(jnp.bfloat16)

    mine = copies_to_chips(pre_grad_own)
    other = core_swap(mine)
    partial = join_cores(
        contract_last(mine, w_in).astype(jnp.bfloat16),
        contract_last(other, w_in).astype(jnp.bfloat16),
    )
    hidden_pair, partial = lax.optimization_barrier((hidden_pair, partial))
    blocks = lax.all_to_all(partial, SECTION, 0, 0, tiled=True)
    input_grad = jnp.sum(blocks.reshape(32, 24, 512).astype(jnp.float32), axis=0)

    hidden_mine = lax.all_gather(hidden_pair, "x", axis=0, tiled=True)
    hidden_mine, mine, other, inputs = lax.optimization_barrier((hidden_mine, mine, other, inputs))
    hidden_other = core_swap(hidden_mine)
    inputs_mine, inputs_other = split_cores(inputs)
    w_in_total = contract_first(inputs_mine, mine) + contract_first(inputs_other, other)
    w_out_total = contract_first(hidden_mine, grad_mine) + contract_first(hidden_other, grad_other)
    return (
        input_grad.astype(jnp.bfloat16),
        w_in_total.astype(jnp.bfloat16),
        w_out_total.astype(jnp.bfloat16),
    )


def solution(mesh):
    cut = Mesh(mesh.devices.reshape(8, 4, 4, 2, 2), SECTION + DP)
    placed = (
        P(None, DP),
        P(None, DP),
        P(DP, SECTION),
        P(DP),
        P(DP, SECTION),
        P(SECTION, DP),
    )
    return jax.shard_map(
        body,
        mesh=cut,
        in_specs=placed,
        out_specs=(P(SECTION, DP), P(DP, SECTION), P(SECTION, DP)),
        check_vma=False,
    )
```

```python
import math

import jax
import jax.numpy as jnp
from jax import lax
from jax.sharding import Mesh
from jax.sharding import PartitionSpec as P

inv_root_two = 1.0 / math.sqrt(2.0)
inv_root_tau = 1.0 / math.sqrt(2.0 * math.pi)

SECTION = ("y", "zh")
CHIPS = ("x", "zl")
DP = ("x", "zl", "core")


def contract_last(left, right):
    return lax.dot_general(
        left, right, (((1,), (1,)), ((), ())), preferred_element_type=jnp.float32
    )


def contract_first(left, right):
    return lax.dot_general(
        left, right, (((0,), (0,)), ((), ())), preferred_element_type=jnp.float32
    )


def core_swap(block):
    return lax.ppermute(block, "core", [(0, 1), (1, 0)])


def split_cores(rows):
    me = lax.axis_index("core")
    cut = rows.reshape(8, 2, 48, rows.shape[1])
    mine = lax.dynamic_index_in_dim(cut, me, 1, keepdims=False)
    other = lax.dynamic_index_in_dim(cut, 1 - me, 1, keepdims=False)
    return mine.reshape(384, -1), other.reshape(384, -1)


def join_cores(mine, other):
    first = lax.axis_index("core") == 0
    mine, other = mine.reshape(8, 48, -1), other.reshape(8, 48, -1)
    both = jnp.stack([jnp.where(first, mine, other), jnp.where(first, other, mine)], axis=1)
    return both.reshape(768, -1)


def copies_to_chips(block):
    return lax.all_to_all(jnp.tile(block, (8, 1)), CHIPS, 0, 0, tiled=True)


def body(inputs, out_grad, saved_codes, row_scale, w_in, w_out):
    pre_act = saved_codes.astype(jnp.float32) * row_scale[:, None]
    normal_cdf = 0.5 * (1.0 + jax.scipy.special.erf(pre_act * inv_root_two))
    hidden_own = (pre_act * normal_cdf).astype(jnp.bfloat16)
    slope_own = (normal_cdf + pre_act * jnp.exp(-0.5 * pre_act * pre_act) * inv_root_tau).astype(
        jnp.bfloat16
    )
    hidden_own, slope_own = lax.optimization_barrier((hidden_own, slope_own))

    grad_mine, grad_other = split_cores(out_grad)
    received = core_swap(contract_last(grad_other, w_out).astype(jnp.bfloat16))
    own_sum = lax.optimization_barrier(contract_last(grad_mine, w_out).astype(jnp.bfloat16))
    inputs, grad_mine = lax.optimization_barrier((inputs, grad_mine))
    inputs_mine, inputs_other = split_cores(inputs)
    received, inputs_mine, inputs_other = lax.optimization_barrier(
        (received, inputs_mine, inputs_other)
    )
    chip_sum = own_sum.astype(jnp.float32) + received.astype(jnp.float32)
    blocks = lax.all_to_all(chip_sum.astype(jnp.bfloat16), CHIPS, 0, 0, tiled=True)
    hidden_pair = lax.all_gather(hidden_own, "zl", axis=0, tiled=True)
    blocks, hidden_pair = lax.optimization_barrier((blocks, hidden_pair))
    grad_share = jnp.sum(blocks.reshape(8, 48, 1024).astype(jnp.float32), axis=0)
    pre_grad_own = (grad_share * slope_own).astype(jnp.bfloat16)

    mine = copies_to_chips(pre_grad_own)
    other = core_swap(mine)
    partial = join_cores(
        contract_last(mine, w_in).astype(jnp.bfloat16),
        contract_last(other, w_in).astype(jnp.bfloat16),
    )
    hidden_pair, partial = lax.optimization_barrier((hidden_pair, partial))
    blocks = lax.all_to_all(partial, SECTION, 0, 0, tiled=True)
    input_grad = jnp.sum(blocks.reshape(32, 24, 512).astype(jnp.float32), axis=0)

    hidden_mine = lax.all_gather(hidden_pair, "x", axis=0, tiled=True)
    hidden_other = core_swap(hidden_mine)
    w_in_total = contract_first(inputs_mine, mine) + contract_first(inputs_other, other)
    w_out_total = contract_first(hidden_mine, grad_mine) + contract_first(hidden_other, grad_other)
    return (
        input_grad.astype(jnp.bfloat16),
        w_in_total.astype(jnp.bfloat16),
        w_out_total.astype(jnp.bfloat16),
    )


def solution(mesh):
    cut = Mesh(mesh.devices.reshape(8, 4, 4, 2, 2), SECTION + DP)
    placed = (
        P(None, DP),
        P(None, DP),
        P(DP, SECTION),
        P(DP),
        P(DP, SECTION),
        P(SECTION, DP),
    )
    return jax.shard_map(
        body,
        mesh=cut,
        in_specs=placed,
        out_specs=(P(SECTION, DP), P(DP, SECTION), P(SECTION, DP)),
        check_vma=False,
    )
```

```python
import math

import jax
import jax.numpy as jnp
import numpy as np
from jax import lax
from jax.sharding import Mesh
from jax.sharding import PartitionSpec as P

inv_root_two = 1.0 / math.sqrt(2.0)
inv_root_tau = 1.0 / math.sqrt(2.0 * math.pi)

SECTION = ("y", "zh")
CHIPS = ("x", "zl")
DP = ("x", "zl", "core")


def contract_last(left, right):
    return lax.dot_general(
        left, right, (((1,), (1,)), ((), ())), preferred_element_type=jnp.float32
    )


def contract_first(left, right):
    return lax.dot_general(
        left, right, (((0,), (0,)), ((), ())), preferred_element_type=jnp.float32
    )


def listed_sections():
    index = np.arange(512).reshape(8, 4, 16)[::-1, ::-1]
    return index.reshape(32, 16).T.tolist()


def core_swap(block):
    return lax.ppermute(block, "core", [(0, 1), (1, 0)])


def split_cores(rows):
    me = lax.axis_index("core")
    cut = rows.reshape(8, 2, 48, rows.shape[1])
    mine = lax.dynamic_index_in_dim(cut, me, 1, keepdims=False)
    other = lax.dynamic_index_in_dim(cut, 1 - me, 1, keepdims=False)
    return mine.reshape(384, -1), other.reshape(384, -1)


def join_cores(mine, other):
    first = lax.axis_index("core") == 0
    mine, other = mine.reshape(8, 48, -1), other.reshape(8, 48, -1)
    both = jnp.stack([jnp.where(first, mine, other), jnp.where(first, other, mine)], axis=1)
    return both.reshape(768, -1)


def copies_to_chips(block):
    return lax.all_to_all(jnp.tile(block, (8, 1)), CHIPS, 0, 0, tiled=True)


def body(inputs, out_grad, saved_codes, row_scale, w_in, w_out):
    pre_act = saved_codes.astype(jnp.float32) * row_scale[:, None]
    normal_cdf = 0.5 * (1.0 + jax.scipy.special.erf(pre_act * inv_root_two))
    hidden_own = (pre_act * normal_cdf).astype(jnp.bfloat16)
    slope_own = (normal_cdf + pre_act * jnp.exp(-0.5 * pre_act * pre_act) * inv_root_tau).astype(
        jnp.bfloat16
    )
    hidden_own, slope_own = lax.optimization_barrier((hidden_own, slope_own))

    grad_mine, grad_other = split_cores(out_grad)
    received = core_swap(contract_last(grad_other, w_out).astype(jnp.bfloat16))
    own_sum = lax.optimization_barrier(contract_last(grad_mine, w_out).astype(jnp.bfloat16))
    inputs, grad_mine = lax.optimization_barrier((inputs, grad_mine))
    inputs_mine, inputs_other = split_cores(inputs)
    received, inputs_mine, inputs_other = lax.optimization_barrier(
        (received, inputs_mine, inputs_other)
    )
    chip_sum = own_sum.astype(jnp.float32) + received.astype(jnp.float32)
    blocks = lax.all_to_all(chip_sum.astype(jnp.bfloat16), CHIPS, 0, 0, tiled=True)
    hidden_pair = lax.all_gather(hidden_own, "zl", axis=0, tiled=True)
    blocks, hidden_pair = lax.optimization_barrier((blocks, hidden_pair))
    grad_share = jnp.sum(blocks.reshape(8, 48, 1024).astype(jnp.float32), axis=0)
    pre_grad_own = (grad_share * slope_own).astype(jnp.bfloat16)

    mine = copies_to_chips(pre_grad_own)
    other = core_swap(mine)
    partial = join_cores(
        contract_last(mine, w_in).astype(jnp.bfloat16),
        contract_last(other, w_in).astype(jnp.bfloat16),
    )
    partial = partial.reshape(8, 4, 24, 512)[::-1, ::-1].reshape(768, 512)
    hidden_pair, partial = lax.optimization_barrier((hidden_pair, partial))
    blocks = lax.all_to_all(
        partial, SECTION + DP, 0, 0, tiled=True, axis_index_groups=listed_sections()
    )
    input_grad = jnp.sum(blocks.reshape(32, 24, 512).astype(jnp.float32), axis=0)

    hidden_mine = lax.all_gather(hidden_pair, "x", axis=0, tiled=True)
    hidden_other = core_swap(hidden_mine)
    w_in_total = contract_first(inputs_mine, mine) + contract_first(inputs_other, other)
    w_out_total = contract_first(hidden_mine, grad_mine) + contract_first(hidden_other, grad_other)
    return (
        input_grad.astype(jnp.bfloat16),
        w_in_total.astype(jnp.bfloat16),
        w_out_total.astype(jnp.bfloat16),
    )


def solution(mesh):
    cut = Mesh(mesh.devices.reshape(8, 4, 4, 2, 2), SECTION + DP)
    placed = (
        P(None, DP),
        P(None, DP),
        P(DP, SECTION),
        P(DP),
        P(DP, SECTION),
        P(SECTION, DP),
    )
    return jax.shard_map(
        body,
        mesh=cut,
        in_specs=placed,
        out_specs=(P(SECTION, DP), P(DP, SECTION), P(SECTION, DP)),
        check_vma=False,
    )
```

```python
import math

import jax
import jax.numpy as jnp
import numpy as np
from jax import lax
from jax.sharding import Mesh
from jax.sharding import PartitionSpec as P

inv_root_two = 1.0 / math.sqrt(2.0)
inv_root_tau = 1.0 / math.sqrt(2.0 * math.pi)

SECTION = ("y", "zh")
CHIPS = ("x", "zl")
DP = ("x", "zl", "core")


def contract_last(left, right):
    return lax.dot_general(
        left, right, (((1,), (1,)), ((), ())), preferred_element_type=jnp.float32
    )


def contract_first(left, right):
    return lax.dot_general(
        left, right, (((0,), (0,)), ((), ())), preferred_element_type=jnp.float32
    )


def listed_sections():
    index = np.arange(512).reshape(8, 4, 16)[::-1, ::-1]
    return index.reshape(32, 16).T.tolist()


def core_swap(block):
    return lax.ppermute(block, "core", [(0, 1), (1, 0)])


def split_cores(rows):
    me = lax.axis_index("core")
    cut = rows.reshape(8, 2, 48, rows.shape[1])
    mine = lax.dynamic_index_in_dim(cut, me, 1, keepdims=False)
    other = lax.dynamic_index_in_dim(cut, 1 - me, 1, keepdims=False)
    return mine.reshape(384, -1), other.reshape(384, -1)


def join_cores(mine, other):
    first = lax.axis_index("core") == 0
    mine, other = mine.reshape(8, 48, -1), other.reshape(8, 48, -1)
    both = jnp.stack([jnp.where(first, mine, other), jnp.where(first, other, mine)], axis=1)
    return both.reshape(768, -1)


def copies_to_chips(block):
    return lax.all_to_all(jnp.tile(block, (8, 1)), CHIPS, 0, 0, tiled=True)


def body(inputs, out_grad, saved_codes, row_scale, w_in, w_out):
    pre_act = saved_codes.astype(jnp.float32) * row_scale[:, None]
    normal_cdf = 0.5 * (1.0 + jax.scipy.special.erf(pre_act * inv_root_two))
    hidden_own = (pre_act * normal_cdf).astype(jnp.bfloat16)
    slope_own = (normal_cdf + pre_act * jnp.exp(-0.5 * pre_act * pre_act) * inv_root_tau).astype(
        jnp.bfloat16
    )
    hidden_own, slope_own = lax.optimization_barrier((hidden_own, slope_own))

    grad_mine, grad_other = split_cores(out_grad)
    received = core_swap(contract_last(grad_other, w_out).astype(jnp.bfloat16))
    own_sum = lax.optimization_barrier(contract_last(grad_mine, w_out).astype(jnp.bfloat16))
    inputs, grad_mine = lax.optimization_barrier((inputs, grad_mine))
    inputs_mine, inputs_other = split_cores(inputs)
    received, inputs_mine, inputs_other, hidden_own, slope_own = lax.optimization_barrier(
        (received, inputs_mine, inputs_other, hidden_own, slope_own)
    )
    chip_sum = own_sum.astype(jnp.float32) + received.astype(jnp.float32)
    blocks = lax.all_to_all(chip_sum.astype(jnp.bfloat16), CHIPS, 0, 0, tiled=True)
    grad_share = jnp.sum(blocks.reshape(8, 48, 1024).astype(jnp.float32), axis=0)
    pre_grad_own = (grad_share * slope_own).astype(jnp.bfloat16)

    mine = copies_to_chips(pre_grad_own)
    hidden_pair = lax.all_gather(hidden_own, "zl", axis=0, tiled=True)
    mine, hidden_pair = lax.optimization_barrier((mine, hidden_pair))
    other = core_swap(mine)
    partial = join_cores(
        contract_last(mine, w_in).astype(jnp.bfloat16),
        contract_last(other, w_in).astype(jnp.bfloat16),
    )
    partial = partial.reshape(8, 4, 24, 512)[::-1, ::-1].reshape(768, 512)
    hidden_pair, partial = lax.optimization_barrier((hidden_pair, partial))
    blocks = lax.all_to_all(
        partial, SECTION + DP, 0, 0, tiled=True, axis_index_groups=listed_sections()
    )
    input_grad = jnp.sum(blocks.reshape(32, 24, 512).astype(jnp.float32), axis=0)

    hidden_mine = lax.all_gather(hidden_pair, "x", axis=0, tiled=True)
    hidden_other = core_swap(hidden_mine)
    w_in_total = contract_first(inputs_mine, mine) + contract_first(inputs_other, other)
    w_out_total = contract_first(hidden_mine, grad_mine) + contract_first(hidden_other, grad_other)
    return (
        input_grad.astype(jnp.bfloat16),
        w_in_total.astype(jnp.bfloat16),
        w_out_total.astype(jnp.bfloat16),
    )


def solution(mesh):
    cut = Mesh(mesh.devices.reshape(8, 4, 4, 2, 2), SECTION + DP)
    placed = (
        P(None, DP),
        P(None, DP),
        P(DP, SECTION),
        P(DP),
        P(DP, SECTION),
        P(SECTION, DP),
    )
    return jax.shard_map(
        body,
        mesh=cut,
        in_specs=placed,
        out_specs=(P(SECTION, DP), P(DP, SECTION), P(SECTION, DP)),
        check_vma=False,
    )
```

```python
import math

import jax
import jax.numpy as jnp
import numpy as np
from jax import lax
from jax.sharding import Mesh
from jax.sharding import PartitionSpec as P

inv_root_two = 1.0 / math.sqrt(2.0)
inv_root_tau = 1.0 / math.sqrt(2.0 * math.pi)

SECTION = ("y", "zh")
CHIPS = ("x", "zl")
DP = ("x", "zl", "core")


def contract_last(left, right):
    return lax.dot_general(
        left, right, (((1,), (1,)), ((), ())), preferred_element_type=jnp.float32
    )


def contract_first(left, right):
    return lax.dot_general(
        left, right, (((0,), (0,)), ((), ())), preferred_element_type=jnp.float32
    )


def listed_sections():
    index = np.arange(512).reshape(8, 4, 16)[::-1, ::-1]
    return index.reshape(32, 16).T.tolist()


def core_swap(block):
    return lax.ppermute(block, "core", [(0, 1), (1, 0)])


def split_cores(rows):
    me = lax.axis_index("core")
    cut = rows.reshape(8, 2, 48, rows.shape[1])
    mine = lax.dynamic_index_in_dim(cut, me, 1, keepdims=False)
    other = lax.dynamic_index_in_dim(cut, 1 - me, 1, keepdims=False)
    return mine.reshape(384, -1), other.reshape(384, -1)


def join_cores(mine, other):
    first = lax.axis_index("core") == 0
    mine, other = mine.reshape(8, 48, -1), other.reshape(8, 48, -1)
    both = jnp.stack([jnp.where(first, mine, other), jnp.where(first, other, mine)], axis=1)
    return both.reshape(768, -1)


def body(inputs, out_grad, saved_codes, row_scale, w_in, w_out):
    pre_act = saved_codes.astype(jnp.float32) * row_scale[:, None]
    normal_cdf = 0.5 * (1.0 + jax.scipy.special.erf(pre_act * inv_root_two))
    hidden_own = (pre_act * normal_cdf).astype(jnp.bfloat16)
    slope_own = (normal_cdf + pre_act * jnp.exp(-0.5 * pre_act * pre_act) * inv_root_tau).astype(
        jnp.bfloat16
    )
    hidden_own, slope_own = lax.optimization_barrier((hidden_own, slope_own))

    grad_mine, grad_other = split_cores(out_grad)
    received = core_swap(contract_last(grad_other, w_out).astype(jnp.bfloat16))
    own_sum = lax.optimization_barrier(contract_last(grad_mine, w_out).astype(jnp.bfloat16))
    inputs, grad_mine = lax.optimization_barrier((inputs, grad_mine))
    inputs_mine, inputs_other = split_cores(inputs)
    slopes = jnp.broadcast_to(slope_own[None], (8, 48, 1024))
    received, inputs_mine, inputs_other, hidden_own, slopes = lax.optimization_barrier(
        (received, inputs_mine, inputs_other, hidden_own, slopes)
    )
    chip_sum = own_sum.astype(jnp.float32) + received.astype(jnp.float32)
    blocks = lax.all_to_all(chip_sum.astype(jnp.bfloat16), CHIPS, 0, 0, tiled=True)
    grad_share = jnp.sum(blocks.reshape(8, 48, 1024).astype(jnp.float32), axis=0)
    pre_grad_copies = (grad_share[None] * slopes).astype(jnp.bfloat16).reshape(384, 1024)

    mine = lax.all_to_all(pre_grad_copies, CHIPS, 0, 0, tiled=True)
    hidden_pair = lax.all_gather(hidden_own, "zl", axis=0, tiled=True)
    mine, hidden_pair = lax.optimization_barrier((mine, hidden_pair))
    other = core_swap(mine)
    partial = join_cores(
        contract_last(mine, w_in).astype(jnp.bfloat16),
        contract_last(other, w_in).astype(jnp.bfloat16),
    )
    partial = partial.reshape(8, 4, 24, 512)[::-1, ::-1].reshape(768, 512)
    hidden_pair, partial = lax.optimization_barrier((hidden_pair, partial))
    blocks = lax.all_to_all(
        partial, SECTION + DP, 0, 0, tiled=True, axis_index_groups=listed_sections()
    )
    input_grad = jnp.sum(blocks.reshape(32, 24, 512).astype(jnp.float32), axis=0)

    hidden_mine = lax.all_gather(hidden_pair, "x", axis=0, tiled=True)
    hidden_other = core_swap(hidden_mine)
    w_in_total = contract_first(inputs_mine, mine) + contract_first(inputs_other, other)
    w_out_total = contract_first(hidden_mine, grad_mine) + contract_first(hidden_other, grad_other)
    return (
        input_grad.astype(jnp.bfloat16),
        w_in_total.astype(jnp.bfloat16),
        w_out_total.astype(jnp.bfloat16),
    )


def solution(mesh):
    cut = Mesh(mesh.devices.reshape(8, 4, 4, 2, 2), SECTION + DP)
    placed = (
        P(None, DP),
        P(None, DP),
        P(DP, SECTION),
        P(DP),
        P(DP, SECTION),
        P(SECTION, DP),
    )
    return jax.shard_map(
        body,
        mesh=cut,
        in_specs=placed,
        out_specs=(P(SECTION, DP), P(DP, SECTION), P(SECTION, DP)),
        check_vma=False,
    )
```
